512 devices in a mesh: section: 32 (over z, x_hi, core), tensor: 16 (over x_lo, y).
Axes of the slice: x: 4 (x_hi: 2, x_lo: 2; x = x_hi * 2 + x_lo), y: 8, z: 8, core: 2. Of those that a mesh axis runs over, the one named last changes fastest.
Arguments:
- fwd_qkv: bfloat16 [32, 3, 480, 6144], P('section', None, None, 'tensor'), may hold values from -4 to 4
- stash: bfloat16 [32, 1, 3, 480, 6144], P('section', None, None, None, 'tensor'), may hold values from -4 to 4
- out_grad: bfloat16 [32, 480, 6144], P('section', None, 'tensor'), may hold values from -6 to 6
- norm_gain: float32 [6144], P('tensor'), may hold values from 0.1 to 1.9
- read_slot: int32 [32], replicated, may hold values from 0 to 1
- write_slot: int32 [32], replicated, may hold values from 0 to 1, as said below
Outputs:
- handed_act: bfloat16 [32, 480, 6144], P('section', None, 'tensor')
- handed_grad: bfloat16 [32, 3, 480, 6144], P('section', None, None, 'tensor')
- new_stash: bfloat16 [32, 1, 3, 480, 6144], P('section', None, None, None, 'tensor')
The draws below stay inside these ranges and needn't reach their ends.
Inputs may be any that keep to these rules, and one draw needn't show every extreme that they name: `write_slot`: the two sections of a pair, p and 31 - p, always name different slots.
All inputs are finite; a program needn't handle non-finite values.
Results may differ from the reference program's by a relative error of at most 0.015.
Values may be sent and summed in bfloat16 or wider, within the bound.
A program may use at most 64 MiB of HBM per device.

```python
import jax
import jax.numpy as jnp
from jax import lax

L = 480
HD = 128
SLOTS = 1
W = 6144
N_SECTION = 32


def draw_fwd_qkv(key, part):
    key = jax.random.fold_in(key, 11)
    dims = (N_SECTION, 3, L, W)
    sample = jnp.clip(jax.random.normal(key, dims, jnp.float32), -4.0, 4.0)
    return sample.astype(jnp.bfloat16)


def draw_stash(key, part):
    key = jax.random.fold_in(key, 12)
    dims = (N_SECTION, SLOTS, 3, L, W)
    sample = jnp.clip(jax.random.normal(key, dims, jnp.float32), -4.0, 4.0)
    return sample.astype(jnp.bfloat16)


def draw_write_slot(key, part):
    key = jax.random.fold_in(key, 13)
    pair_keys = jax.random.split(key, N_SECTION // 2)
    orders = jax.vmap(lambda single: jax.random.permutation(single, 2 * SLOTS))(pair_keys)
    lower_pick = orders[:, 0].at[0].set(0)
    upper_pick = orders[:, 1].at[0].set(2 * SLOTS - 1)
    return jnp.concatenate([lower_pick, upper_pick[::-1]]).astype(jnp.int32)


def with_ends(array, stream_key, smallest, largest):
    longest = array.shape.index(max(array.shape))
    spots = []
    for shift in (0, 1):
        where = [jax.random.randint(jax.random.fold_in(stream_key, axis), (), 0, length) for axis, length in enumerate(array.shape)]
        where[longest] = (where[longest] + shift) % array.shape[longest]
        spots.append(tuple(where))
    return array.at[spots[0]].set(smallest).at[spots[1]].set(largest)


def block_scale(own_key, shape, cuts, least, high):
    gain = 1.0
    for axis_at, parts in cuts:
        steps = jax.random.uniform(jax.random.fold_in(jax.random.fold_in(own_key, 6), axis_at), (parts,), jnp.float32, least / len(cuts), high / len(cuts))
        gain = gain * jnp.repeat(jnp.exp(steps), shape[axis_at] // parts).reshape((-1,) + (1,) * (len(shape) - 1 - axis_at))
    return gain


def scatter_about(own_key, extent, scale, reach, shards=(), kind=jnp.bfloat16):
    entries = scale * jax.random.normal(own_key, extent, jnp.float32)
    if shards:
        entries = entries * block_scale(own_key, extent, shards, -0.22, 0.18)
    return jnp.clip(entries, -reach, reach).astype(kind)


def setup_inputs(seed: int = 0) -> dict:
    key_of = jax.random.split(jax.random.key(seed), 7)
    return {
        "fwd_qkv": draw_fwd_qkv(jax.random.fold_in(key_of[6], 71), 0),
        "stash": draw_stash(jax.random.fold_in(key_of[6], 71), 0),
        "out_grad": scatter_about(key_of[2], (N_SECTION, L, W), 1.0, 6.0, ((0, 32), (2, 16))),
        "norm_gain": jnp.clip(1.0 + 0.18 * jax.random.normal(key_of[3], (W,), jnp.float32), 0.1, 1.9),
        "read_slot": with_ends(jax.random.randint(key_of[4], (N_SECTION,), 0, 2 * SLOTS), jax.random.fold_in(key_of[4], 1), 0, (2 * SLOTS) - 1).astype(jnp.int32),
        "write_slot": draw_write_slot(jax.random.fold_in(key_of[6], 71), 0),
    }


NORM_EPS = 1e-05

def attend(query, keys_in, values_in):
    length = query.shape[0]
    q_heads = query.astype(jnp.float32).reshape(length, -1, HD)
    k_heads = keys_in.astype(jnp.float32).reshape(length, -1, HD)
    v_heads = values_in.astype(jnp.float32).reshape(length, -1, HD)
    scores = jnp.einsum('qhd,khd->hqk', q_heads, k_heads) * HD ** (-0.5)
    positions = jnp.arange(length, dtype=jnp.int32)
    causal = positions[:, None] >= positions[None, :]
    scores = jnp.where(causal[None], scores, jnp.float32(-1e+30))
    top_score = lax.optimization_barrier(jnp.max(scores, axis=-1, keepdims=True))
    exp_terms = jnp.exp(scores - top_score)
    soft_probs = exp_terms / lax.optimization_barrier(jnp.sum(exp_terms, axis=-1, keepdims=True))
    probs_low = soft_probs.astype(jnp.bfloat16)
    attended = jnp.einsum('hqk,khd->qhd', probs_low.astype(jnp.float32), v_heads).reshape(length, -1)
    return (soft_probs, probs_low, attended)

def attend_back(query, keys_in, values_in, soft_probs, probs_low, attended, grad_att):
    length = query.shape[0]
    q_heads = query.astype(jnp.float32).reshape(length, -1, HD)
    k_heads = keys_in.astype(jnp.float32).reshape(length, -1, HD)
    v_heads = values_in.astype(jnp.float32).reshape(length, -1, HD)
    g_heads = grad_att.astype(jnp.float32).reshape(length, -1, HD)
    a_heads = attended.reshape(length, -1, HD)
    grad_probs = jnp.einsum('qhd,khd->hqk', g_heads, v_heads)
    grad_values = jnp.einsum('hqk,qhd->khd', probs_low.astype(jnp.float32), g_heads)
    row_delta = jnp.transpose(lax.optimization_barrier(jnp.sum(g_heads * a_heads, axis=-1)))
    grad_scores = (soft_probs * (grad_probs - row_delta[:, :, None]) * HD ** (-0.5)).astype(jnp.bfloat16)
    grad_query = jnp.einsum('hqk,khd->qhd', grad_scores.astype(jnp.float32), k_heads)
    grad_keys = jnp.einsum('hqk,qhd->khd', grad_scores.astype(jnp.float32), q_heads)
    stacked = jnp.stack([grad_query.astype(jnp.bfloat16), grad_keys.astype(jnp.bfloat16), grad_values.astype(jnp.bfloat16)])
    return stacked.reshape(3, length, -1)

def reference(fwd_qkv, stash, out_grad, norm_gain, read_slot, write_slot):
    sections = jnp.arange(N_SECTION, dtype=jnp.int32)
    partner = N_SECTION - 1 - sections
    lower_member = jnp.minimum(sections, partner)
    upper_member = jnp.maximum(sections, partner)
    holder = jnp.where(read_slot < SLOTS, lower_member, upper_member)
    fetched = stash[holder, read_slot % SLOTS]

    def one_section(section_items):
        forward_in, backward_in, grad_in = section_items
        unused_a, unused_b, out_fwd = attend(forward_in[0], forward_in[1], forward_in[2])
        inv_fwd = lax.rsqrt(lax.optimization_barrier(jnp.mean(out_fwd * out_fwd, axis=-1)) + NORM_EPS)
        handed = (out_fwd * inv_fwd[:, None] * norm_gain).astype(jnp.bfloat16)
        soft_probs, probs_low, out_back = attend(backward_in[0], backward_in[1], backward_in[2])
        inv_back = lax.rsqrt(lax.optimization_barrier(jnp.mean(out_back * out_back, axis=-1)) + NORM_EPS)
        scaled_grad = grad_in.astype(jnp.float32) * norm_gain
        row_dot = lax.optimization_barrier(jnp.mean(scaled_grad * out_back, axis=-1))
        grad_att = (inv_back[:, None] * scaled_grad - out_back * (inv_back ** 3 * row_dot)[:, None]).astype(jnp.bfloat16)
        grads = attend_back(backward_in[0], backward_in[1], backward_in[2], soft_probs, probs_low, out_back, grad_att)
        return (handed, grads)
    acts, grads = lax.map(one_section, (fwd_qkv, fetched, out_grad))
    handed_act = jnp.concatenate([jnp.zeros((1, L, W), jnp.bfloat16), acts[:-1]], axis=0)
    handed_grad = jnp.concatenate([grads[1:], jnp.zeros((1, 3, L, W), jnp.bfloat16)], axis=0)
    writer_holder = jnp.where(write_slot < SLOTS, lower_member, upper_member)
    new_stash = stash.at[writer_holder, write_slot % SLOTS].set(fwd_qkv)
    return (handed_act, handed_grad, new_stash)
```

```python
import functools

import jax
import jax.numpy as jnp
from jax import lax
from jax.experimental import pallas as pl
from jax.experimental.pallas import tpu as pltpu
from jax.sharding import PartitionSpec as P

HD = 128
NORM_EPS = 1e-05
SCALE = HD ** (-0.5)
MESH = pl.DeviceIdType.MESH
F32 = jnp.float32
BF16 = jnp.bfloat16


def cols(head):
    return pl.ds(head * HD, HD)


def nt(a, b):
    return lax.dot_general(a, b, (((1,), (1,)), ((), ())), preferred_element_type=F32)


def nn(a, b):
    return lax.dot_general(a, b, (((1,), (0,)), ((), ())), preferred_element_type=F32)


def tn(a, b):
    return lax.dot_general(a, b, (((0,), (0,)), ((), ())), preferred_element_type=F32)


def attend(q, k, v):
    length = q.shape[0]
    scores = nt(q, k) * SCALE
    rows = lax.broadcasted_iota(jnp.int32, (length, length), 0)
    keys = lax.broadcasted_iota(jnp.int32, (length, length), 1)
    scores = jnp.where(rows >= keys, scores, F32(-1e30))
    terms = jnp.exp(scores - jnp.max(scores, axis=-1, keepdims=True))
    probs = terms * (1.0 / jnp.sum(terms, axis=-1, keepdims=True))
    low = probs.astype(BF16)
    return probs, low, nn(low, v)


def kernel(
    n_sec, n_ten, width_all,
    flags_ref, fwd_ref, stash_ref, og_ref, gain_ref,
    act_ref, grad_ref, new_ref,
    got_s, got_f, act_out, grad_out, att_f, att_b, probs_ref, low_ref, part, wide, tiles_f, tiles_b,
    s_send, s_recv, f_send, f_recv, g_send, g_recv, a_send, a_recv, pf_send, pf_recv, pb_send, pb_recv,
):
    length = og_ref.shape[0]
    heads = og_ref.shape[1] // HD
    me_s = lax.axis_index("section")
    me_t = lax.axis_index("tensor")
    partner = (n_sec - 1 - me_s, me_t)
    up = (me_s + 1, me_t)
    down = (me_s - 1, me_t)
    has_up = me_s < n_sec - 1
    has_down = me_s > 0

    barrier = pltpu.get_barrier_semaphore()

    def greet(device):
        pl.semaphore_signal(barrier, inc=1, device_id=device, device_id_type=MESH)

    greet(partner)
    greet((lax.rem(me_s + 1, n_sec), me_t))
    greet((lax.rem(me_s + n_sec - 1, n_sec), me_t))

    def greet_peer(step, carry):
        greet((me_s, lax.rem(me_t + step, n_ten)))
        return carry

    lax.fori_loop(1, n_ten, greet_peer, 0)
    pl.semaphore_wait(barrier, n_ten + 2)

    def copy_to(src, dst, send, recv, device):
        return pltpu.make_async_remote_copy(
            src_ref=src, dst_ref=dst, send_sem=send, recv_sem=recv, device_id=device, device_id_type=MESH
        )

    def stash_copy(h):
        return copy_to(
            stash_ref.at[:, :, cols(h)], got_s.at[:, :, cols(h)], s_send.at[h], s_recv.at[h], partner
        )

    def fwd_copy(h):
        return copy_to(
            fwd_ref.at[:, :, cols(h)], got_f.at[:, :, cols(h)], f_send.at[h], f_recv.at[h], partner
        )

    def grad_copy(h):
        return copy_to(
            grad_out.at[:, :, cols(h)], grad_ref.at[:, :, cols(h)], g_send.at[h], g_recv.at[h], down
        )

    def act_copy():
        return copy_to(act_out, act_ref, a_send.at[0], a_recv.at[0], up)

    def spread(tiles, send, recv):
        def start(step, carry):
            peer = lax.rem(me_t + step, n_ten)
            copy_to(tiles.at[me_t], tiles.at[me_t], send.at[step], recv.at[me_t], (me_s, peer)).start()
            return carry

        lax.fori_loop(1, n_ten, start, 0)

    def collect(tiles, send, recv):
        def finish(step, carry):
            peer = lax.rem(me_t + step, n_ten)
            copy_to(tiles.at[me_t], tiles.at[me_t], send.at[step], recv.at[me_t], (me_s, peer)).wait_send()
            copy_to(tiles.at[peer], tiles.at[peer], send.at[step], recv.at[peer], (me_s, peer)).wait_recv()
            return carry

        lax.fori_loop(1, n_ten, finish, 0)
        return jnp.sum(tiles[...], axis=0)

    def token_sums(tile, row, partial):
        wide[0:length, :] = partial
        for block in range(4):
            summed = jnp.sum(jnp.transpose(wide[block * HD : (block + 1) * HD, :]), axis=0, keepdims=True)
            tile[row + block : row + block + 1, :] = summed

    def per_token(rows):
        blocks = [
            jnp.transpose(jnp.broadcast_to(rows[b : b + 1, :], (HD, HD))) for b in range(4)
        ]
        return jnp.concatenate(blocks, axis=0)[0:length, :]

    for h in range(heads):
        stash_copy(h).start()

    wide[...] = jnp.zeros_like(wide)
    tiles_f[me_t] = jnp.zeros((8, HD), F32)

    squares = jnp.zeros((length, HD), F32)
    for h in range(heads):
        unused_a, unused_b, out = attend(fwd_ref[0, :, cols(h)], fwd_ref[1, :, cols(h)], fwd_ref[2, :, cols(h)])
        att_f[:, cols(h)] = out
        squares += out * out
    token_sums(part, 0, squares)
    tiles_f[me_t, 0:4, :] = part[0:4, :]
    spread(tiles_f, pf_send, pf_recv)
    total = collect(tiles_f, pf_send, pf_recv)
    inv_fwd = per_token(lax.rsqrt(total[0:4, :] / width_all + NORM_EPS))
    for h in range(heads):
        act_out[:, cols(h)] = (att_f[:, cols(h)] * inv_fwd * gain_ref[0:1, cols(h)]).astype(BF16)
    pl.when(has_up)(lambda: act_copy().start())

    @pl.when(jnp.logical_not(has_down))
    def _():
        act_ref[...] = jnp.zeros_like(act_ref)

    @pl.when(jnp.logical_not(has_up))
    def _():
        grad_ref[...] = jnp.zeros_like(grad_ref)

    own_read = flags_ref[0] > 0
    own_write = flags_ref[1] > 0
    squares = jnp.zeros((length, HD), F32)
    products = jnp.zeros((length, HD), F32)
    for h in range(heads):
        stash_copy(h).wait()
        if h == heads - 1:
            for other in range(heads):
                fwd_copy(other).start()
        for part_at in range(3):
            got_s[part_at, :, cols(h)] = jnp.where(
                own_read, stash_ref[part_at, :, cols(h)], got_s[part_at, :, cols(h)]
            )
        probs, low, out = attend(got_s[0, :, cols(h)], got_s[1, :, cols(h)], got_s[2, :, cols(h)])
        probs_ref[h] = probs
        low_ref[h] = low
        att_b[:, cols(h)] = out
        squares += out * out
        products += og_ref[:, cols(h)].astype(F32) * gain_ref[0:1, cols(h)] * out
    token_sums(part, 0, squares)
    token_sums(part, 4, products)
    tiles_b[me_t] = part[...]
    spread(tiles_b, pb_send, pb_recv)
    total = collect(tiles_b, pb_send, pb_recv)
    inv = lax.rsqrt(total[0:4, :] / width_all + NORM_EPS)
    inv_back = per_token(inv)
    pull = per_token(inv * inv * inv * (total[4:8, :] / width_all))
    for h in range(heads):
        out = att_b[:, cols(h)]
        scaled = og_ref[:, cols(h)].astype(F32) * gain_ref[0:1, cols(h)]
        g_low = (inv_back * scaled - out * pull).astype(BF16)
        grad_probs = nt(g_low, got_s[2, :, cols(h)])
        delta = jnp.sum(g_low.astype(F32) * out, axis=-1, keepdims=True)
        grad_scores = (probs_ref[h] * (grad_probs - delta) * SCALE).astype(BF16)
        grad_out[0, :, cols(h)] = nn(grad_scores, got_s[1, :, cols(h)]).astype(BF16)
        grad_out[1, :, cols(h)] = tn(grad_scores, got_s[0, :, cols(h)]).astype(BF16)
        grad_out[2, :, cols(h)] = tn(low_ref[h], g_low).astype(BF16)
        pl.when(has_down)(lambda: grad_copy(h).start())

    for h in range(heads):
        fwd_copy(h).wait()
        for part_at in range(3):
            new_ref[part_at, :, cols(h)] = jnp.where(
                own_write, fwd_ref[part_at, :, cols(h)], got_f[part_at, :, cols(h)]
            )

    @pl.when(has_up)
    def _():
        act_copy().wait_send()
        for h in range(heads):
            grad_copy(h).wait_recv()

    @pl.when(has_down)
    def _():
        act_copy().wait_recv()
        for h in range(heads):
            grad_copy(h).wait_send()


def shards(fwd_qkv, stash, out_grad, norm_gain, read_slot, write_slot):
    n_sec = lax.axis_size("section")
    n_ten = lax.axis_size("tensor")
    here = lax.axis_index("section")
    slot_count = stash.shape[1]
    lower = here < n_sec // 2
    own_read = (read_slot[here] < slot_count) == lower
    own_write = (write_slot[here] < slot_count) == lower
    flags = jnp.stack([own_read, own_write]).astype(jnp.int32)
    three, length, width = fwd_qkv.shape[1:]
    heads = width // HD
    dma = pltpu.SemaphoreType.DMA
    vmem = pl.BlockSpec(memory_space=pltpu.VMEM)
    act, grads, new = pl.pallas_call(
        functools.partial(kernel, n_sec, n_ten, float(width * n_ten)),
        out_shape=(
            jax.ShapeDtypeStruct((length, width), BF16),
            jax.ShapeDtypeStruct((three, length, width), BF16),
            jax.ShapeDtypeStruct((three, length, width), BF16),
        ),
        in_specs=[pl.BlockSpec(memory_space=pltpu.SMEM)] + [vmem] * 4,
        out_specs=(vmem, vmem, vmem),
        scratch_shapes=[
            pltpu.VMEM((three, length, width), BF16),
            pltpu.VMEM((three, length, width), BF16),
            pltpu.VMEM((length, width), BF16),
            pltpu.VMEM((three, length, width), BF16),
            pltpu.VMEM((length, width), F32),
            pltpu.VMEM((length, width), F32),
            pltpu.VMEM((heads, length, length), F32),
            pltpu.VMEM((heads, length, length), BF16),
            pltpu.VMEM((8, HD), F32),
            pltpu.VMEM((4 * HD, HD), F32),
            pltpu.VMEM((n_ten, 8, HD), F32),
            pltpu.VMEM((n_ten, 8, HD), F32),
            dma((heads,)), dma((heads,)), dma((heads,)), dma((heads,)), dma((heads,)), dma((heads,)),
            dma((1,)), dma((1,)),
            dma((n_ten,)), dma((n_ten,)), dma((n_ten,)), dma((n_ten,)),
        ],
        compiler_params=pltpu.CompilerParams(
            collective_id=0, has_side_effects=True, vmem_limit_bytes=48 * 1024 * 1024
        ),
        name="slot",
    )(flags, fwd_qkv[0], stash[0, 0], out_grad[0], norm_gain[None])
    return act[None], grads[None], new[None, None]


def solution(mesh):
    in_specs = (
        P("section", None, None, "tensor"),
        P("section", None, None, None, "tensor"),
        P("section", None, "tensor"),
        P("tensor"),
        P(),
        P(),
    )
    out_specs = (
        P("section", None, "tensor"),
        P("section", None, None, "tensor"),
        P("section", None, None, None, "tensor"),
    )
    return jax.shard_map(shards, mesh=mesh, in_specs=in_specs, out_specs=out_specs, check_vma=False)
```

```python
import functools

import jax
import jax.numpy as jnp
from jax import lax
from jax.experimental import pallas as pl
from jax.experimental.pallas import tpu as pltpu
from jax.sharding import PartitionSpec as P

HD = 128
NORM_EPS = 1e-05
SCALE = HD ** (-0.5)
PER_Z = 4
MESH = pl.DeviceIdType.MESH
F32 = jnp.float32
BF16 = jnp.bfloat16


def cols(head):
    return pl.ds(head * HD, HD)


def nt(a, b):
    return lax.dot_general(a, b, (((1,), (1,)), ((), ())), preferred_element_type=F32)


def nn(a, b):
    return lax.dot_general(a, b, (((1,), (0,)), ((), ())), preferred_element_type=F32)


def tn(a, b):
    return lax.dot_general(a, b, (((0,), (0,)), ((), ())), preferred_element_type=F32)


def attend(q, k, v):
    length = q.shape[0]
    scores = nt(q, k) * SCALE
    rows = lax.broadcasted_iota(jnp.int32, (length, length), 0)
    keys = lax.broadcasted_iota(jnp.int32, (length, length), 1)
    scores = jnp.where(rows >= keys, scores, F32(-1e30))
    terms = jnp.exp(scores - jnp.max(scores, axis=-1, keepdims=True))
    probs = terms * (1.0 / jnp.sum(terms, axis=-1, keepdims=True))
    low = probs.astype(BF16)
    return probs, low, nn(low, v)


def kernel(
    n_sec, n_ten, width_all,
    read_in, write_in, fwd_in, stash_in, og_in, gain_in,
    act_ref, grad_ref, new_out,
    new_ref, zeros, read_ref, write_ref, gain_ref, fwd_ref, stash_ref, og_ref, got_s, got_f, act_out, grad_out, att_f, att_b, probs_ref, low_ref, part, wide, tiles_f, tiles_b,
    s_send, s_recv, f_send, f_recv, g_send, g_recv, a_send, a_recv, pf_send, pf_recv, pb_send, pb_recv, loads, go_sem,
):
    length = og_ref.shape[0]
    heads = og_ref.shape[1] // HD
    me_s = lax.axis_index("section")
    me_t = lax.axis_index("tensor")
    partner = (n_sec - 1 - me_s, me_t)
    up = (me_s + 1, me_t)
    down = (me_s - 1, me_t)
    has_up = me_s < n_sec - 1
    has_down = me_s > 0
    layer = me_s // PER_Z
    next_to_middle = lax.rem(layer + 1, 4) < 2
    z_mate = (me_s + PER_Z * (1 - 2 * lax.rem(layer, 2)), me_t)

    load_stash = pltpu.make_async_copy(stash_in, stash_ref, loads.at[0])
    load_fwd = pltpu.make_async_copy(fwd_in, fwd_ref, loads.at[1])
    load_og = pltpu.make_async_copy(og_in, og_ref, loads.at[2])
    small = [
        pltpu.make_async_copy(src, dst, loads.at[3 + i])
        for i, (src, dst) in enumerate(((read_in, read_ref), (write_in, write_ref), (gain_in, gain_ref)))
    ]
    load_stash.start()
    load_fwd.start()
    load_og.start()
    for load in small:
        load.start()

    barrier = pltpu.get_barrier_semaphore()

    def greet(device):
        pl.semaphore_signal(barrier, inc=1, device_id=device, device_id_type=MESH)

    greet(partner)
    greet(z_mate)
    greet((lax.rem(me_s + 1, n_sec), me_t))
    greet((lax.rem(me_s + n_sec - 1, n_sec), me_t))

    def greet_peer(step, carry):
        greet((me_s, lax.rem(me_t + step, n_ten)))
        return carry

    lax.fori_loop(1, n_ten, greet_peer, 0)
    load_stash.wait()
    pl.semaphore_wait(barrier, n_ten + 3)

    def copy_to(src, dst, send, recv, device):
        return pltpu.make_async_remote_copy(
            src_ref=src, dst_ref=dst, send_sem=send, recv_sem=recv, device_id=device, device_id_type=MESH
        )

    def stash_copy(h):
        return copy_to(
            stash_ref.at[:, :, cols(h)], got_s.at[:, :, cols(h)], s_send.at[h], s_recv.at[h], partner
        )

    def fwd_copy(h):
        return copy_to(
            fwd_ref.at[:, :, cols(h)], got_f.at[:, :, cols(h)], f_send.at[h], f_recv.at[h], partner
        )

    def grad_copy(h):
        return copy_to(
            grad_out.at[:, :, cols(h)], grad_ref.at[:, :, cols(h)], g_send.at[h], g_recv.at[h], down
        )

    def act_copy():
        return copy_to(act_out, act_ref, a_send.at[0], a_recv.at[0], up)

    def spread(tiles, send, recv):
        def start(step, carry):
            peer = lax.rem(me_t + step, n_ten)
            copy_to(tiles.at[me_t], tiles.at[me_t], send.at[step], recv.at[me_t], (me_s, peer)).start()
            return carry

        lax.fori_loop(1, n_ten, start, 0)

    def collect(tiles, send, recv):
        def finish(step, carry):
            peer = lax.rem(me_t + step, n_ten)
            copy_to(tiles.at[me_t], tiles.at[me_t], send.at[step], recv.at[me_t], (me_s, peer)).wait_send()
            copy_to(tiles.at[peer], tiles.at[peer], send.at[step], recv.at[peer], (me_s, peer)).wait_recv()
            return carry

        lax.fori_loop(1, n_ten, finish, 0)
        return jnp.sum(tiles[...], axis=0)

    def token_sums(tile, row, partial):
        wide[0:length, :] = partial
        for block in range(4):
            summed = jnp.sum(jnp.transpose(wide[block * HD : (block + 1) * HD, :]), axis=0, keepdims=True)
            tile[row + block : row + block + 1, :] = summed

    def per_token(rows):
        blocks = [
            jnp.transpose(jnp.broadcast_to(rows[b : b + 1, :], (HD, HD))) for b in range(4)
        ]
        return jnp.concatenate(blocks, axis=0)[0:length, :]

    for h in range(heads):
        stash_copy(h).start()

    wide[...] = jnp.zeros_like(wide)
    tiles_f[me_t] = jnp.zeros((8, HD), F32)

    load_fwd.wait()
    load_og.wait()
    for load in small:
        load.wait()
    squares = jnp.zeros((length, HD), F32)
    for h in range(heads):
        unused_a, unused_b, out = attend(fwd_ref[0, :, cols(h)], fwd_ref[1, :, cols(h)], fwd_ref[2, :, cols(h)])
        att_f[:, cols(h)] = out
        squares += out * out
    token_sums(part, 0, squares)
    tiles_f[me_t, 0:4, :] = part[0:4, :]
    spread(tiles_f, pf_send, pf_recv)
    total = collect(tiles_f, pf_send, pf_recv)
    inv_fwd = per_token(lax.rsqrt(total[0:4, :] / width_all + NORM_EPS))
    for h in range(heads):
        act_out[:, cols(h)] = (att_f[:, cols(h)] * inv_fwd * gain_ref[cols(h)][None, :]).astype(BF16)
    pl.when(has_up)(lambda: act_copy().start())

    @pl.when(jnp.logical_not(has_down))
    def _():
        zeros[...] = jnp.zeros_like(zeros)
        blank = pltpu.make_async_copy(zeros.at[0], act_ref, loads.at[6])
        blank.start()
        blank.wait()

    @pl.when(jnp.logical_not(has_up))
    def _():
        zeros[...] = jnp.zeros_like(zeros)
        blank = pltpu.make_async_copy(zeros, grad_ref, loads.at[6])
        blank.start()
        blank.wait()

    lower = me_s < n_sec // 2
    own_read = (read_ref[me_s] < 1) == lower
    own_write = (write_ref[me_s] < 1) == lower
    squares = jnp.zeros((length, HD), F32)
    products = jnp.zeros((length, HD), F32)
    for h in range(heads):
        if h == heads - 1:
            for other in range(heads):
                stash_copy(other).wait_send()

            @pl.when(next_to_middle)
            def _():
                pl.semaphore_signal(go_sem, inc=1, device_id=z_mate, device_id_type=MESH)

        stash_copy(h).wait_recv()
        for part_at in range(3):
            got_s[part_at, :, cols(h)] = jnp.where(
                own_read, stash_ref[part_at, :, cols(h)], got_s[part_at, :, cols(h)]
            )
        probs, low, out = attend(got_s[0, :, cols(h)], got_s[1, :, cols(h)], got_s[2, :, cols(h)])
        probs_ref[h] = probs
        low_ref[h] = low
        att_b[:, cols(h)] = out
        squares += out * out
        products += og_ref[:, cols(h)].astype(F32) * gain_ref[cols(h)][None, :] * out
    token_sums(part, 0, squares)
    token_sums(part, 4, products)
    tiles_b[me_t] = part[...]
    spread(tiles_b, pb_send, pb_recv)
    total = collect(tiles_b, pb_send, pb_recv)
    inv = lax.rsqrt(total[0:4, :] / width_all + NORM_EPS)
    inv_back = per_token(inv)
    pull = per_token(inv * inv * inv * (total[4:8, :] / width_all))
    for h in range(heads):
        out = att_b[:, cols(h)]
        scaled = og_ref[:, cols(h)].astype(F32) * gain_ref[cols(h)][None, :]
        g_low = (inv_back * scaled - out * pull).astype(BF16)
        grad_probs = nt(g_low, got_s[2, :, cols(h)])
        delta = jnp.sum(g_low.astype(F32) * out, axis=-1, keepdims=True)
        grad_scores = (probs_ref[h] * (grad_probs - delta) * SCALE).astype(BF16)
        grad_out[0, :, cols(h)] = nn(grad_scores, got_s[1, :, cols(h)]).astype(BF16)
        grad_out[1, :, cols(h)] = tn(grad_scores, got_s[0, :, cols(h)]).astype(BF16)
        grad_out[2, :, cols(h)] = tn(low_ref[h], g_low).astype(BF16)
        pl.when(has_down)(lambda: grad_copy(h).start())

    @pl.when(jnp.logical_not(next_to_middle))
    def _():
        pl.semaphore_wait(go_sem, 1)

    for h in range(heads):
        fwd_copy(h).start()
    for h in range(heads):
        fwd_copy(h).wait()
        for part_at in range(3):
            new_ref[part_at, :, cols(h)] = jnp.where(
                own_write, fwd_ref[part_at, :, cols(h)], got_f[part_at, :, cols(h)]
            )

    store = pltpu.make_async_copy(new_ref, new_out, loads.at[7])
    store.start()

    @pl.when(has_up)
    def _():
        act_copy().wait_send()
        for h in range(heads):
            grad_copy(h).wait_recv()

    @pl.when(has_down)
    def _():
        act_copy().wait_recv()
        for h in range(heads):
            grad_copy(h).wait_send()

    store.wait()


def shards(fwd_qkv, stash, out_grad, norm_gain, read_slot, write_slot):
    n_sec = lax.axis_size("section")
    n_ten = lax.axis_size("tensor")
    three, length, width = fwd_qkv.shape[1:]
    heads = width // HD
    dma = pltpu.SemaphoreType.DMA
    vmem = pl.BlockSpec(memory_space=pltpu.VMEM)
    act, grads, new = pl.pallas_call(
        functools.partial(kernel, n_sec, n_ten, float(width * n_ten)),
        out_shape=(
            jax.ShapeDtypeStruct((length, width), BF16),
            jax.ShapeDtypeStruct((three, length, width), BF16),
            jax.ShapeDtypeStruct((three, length, width), BF16),
        ),
        in_specs=[pl.BlockSpec(memory_space=pl.ANY)] * 6,
        out_specs=(pl.BlockSpec(memory_space=pl.ANY),) * 3,
        scratch_shapes=[
            pltpu.VMEM((three, length, width), BF16),
            pltpu.VMEM((three, length, width), BF16),
            pltpu.SMEM(read_slot.shape, jnp.int32),
            pltpu.SMEM(write_slot.shape, jnp.int32),
            pltpu.VMEM(norm_gain.shape, F32),
            pltpu.VMEM((three, length, width), BF16),
            pltpu.VMEM((three, length, width), BF16),
            pltpu.VMEM((length, width), BF16),
            pltpu.VMEM((three, length, width), BF16),
            pltpu.VMEM((three, length, width), BF16),
            pltpu.VMEM((length, width), BF16),
            pltpu.VMEM((three, length, width), BF16),
            pltpu.VMEM((length, width), F32),
            pltpu.VMEM((length, width), F32),
            pltpu.VMEM((heads, length, length), F32),
            pltpu.VMEM((heads, length, length), BF16),
            pltpu.VMEM((8, HD), F32),
            pltpu.VMEM((4 * HD, HD), F32),
            pltpu.VMEM((n_ten, 8, HD), F32),
            pltpu.VMEM((n_ten, 8, HD), F32),
            dma((heads,)), dma((heads,)), dma((heads,)), dma((heads,)), dma((heads,)), dma((heads,)),
            dma((1,)), dma((1,)),
            dma((n_ten,)), dma((n_ten,)), dma((n_ten,)), dma((n_ten,)),
            dma((8,)), pltpu.SemaphoreType.REGULAR,
        ],
        compiler_params=pltpu.CompilerParams(
            collective_id=0, has_side_effects=True, vmem_limit_bytes=56 * 1024 * 1024
        ),
        name="slot",
    )(read_slot, write_slot, fwd_qkv[0], stash[0, 0], out_grad[0], norm_gain)
    return act[None], grads[None], new[None, None]


def solution(mesh):
    in_specs = (
        P("section", None, None, "tensor"),
        P("section", None, None, None, "tensor"),
        P("section", None, "tensor"),
        P("tensor"),
        P(),
        P(),
    )
    out_specs = (
        P("section", None, "tensor"),
        P("section", None, None, "tensor"),
        P("section", None, None, None, "tensor"),
    )
    return jax.shard_map(shards, mesh=mesh, in_specs=in_specs, out_specs=out_specs, check_vma=False)
```

```python
import functools

import jax
import jax.numpy as jnp
from jax import lax
from jax.experimental import pallas as pl
from jax.experimental.pallas import tpu as pltpu
from jax.sharding import PartitionSpec as P

HD = 128
NORM_EPS = 1e-05
SCALE = HD ** (-0.5)
PER_Z = 4
PART = 128
LEAST = 2
MESH = pl.DeviceIdType.MESH
F32 = jnp.float32
BF16 = jnp.bfloat16


def cols(head):
    return pl.ds(head * HD, HD)


def nt(a, b):
    return lax.dot_general(a, b, (((1,), (1,)), ((), ())), preferred_element_type=F32)


def nn(a, b):
    return lax.dot_general(a, b, (((1,), (0,)), ((), ())), preferred_element_type=F32)


def tn(a, b):
    return lax.dot_general(a, b, (((0,), (0,)), ((), ())), preferred_element_type=F32)


def attend(q, k, v):
    length = q.shape[0]
    scores = nt(q, k) * SCALE
    rows = lax.broadcasted_iota(jnp.int32, (length, length), 0)
    keys = lax.broadcasted_iota(jnp.int32, (length, length), 1)
    scores = jnp.where(rows >= keys, scores, F32(-1e30))
    terms = jnp.exp(scores - jnp.max(scores, axis=-1, keepdims=True))
    probs = terms * (1.0 / jnp.sum(terms, axis=-1, keepdims=True))
    low = probs.astype(BF16)
    return probs, low, nn(low, v)


def kernel(
    n_sec, n_ten, width_all, slots,
    read_in, write_in, fwd_in, stash_in, og_in, gain_in,
    act_ref, grad_ref, new_out,
    new_ref, zeros, read_ref, write_ref, gain_ref, fwd_ref, stash_ref, og_ref, pay_ref, got_s, back_ref, gathered, packed, crossed, fan, quarters, act_out, grad_out, att_f, att_b, probs_ref, low_ref, part, wide, tiles_f, tiles_b,
    s_send, s_recv, q_send, q_recv, c_send, c_recv, d_send, d_recv, g_send, g_recv, a_send, a_recv, pf_send, pf_recv, pb_send, pb_recv, loads, go_sem,
):
    length = og_ref.shape[0]
    heads = og_ref.shape[1] // HD
    me_s = lax.axis_index("section")
    me_t = lax.axis_index("tensor")
    partner = (n_sec - 1 - me_s, me_t)
    up = (me_s + 1, me_t)
    down = (me_s - 1, me_t)
    has_up = me_s < n_sec - 1
    has_down = me_s > 0
    layer = me_s // PER_Z
    next_to_middle = lax.rem(layer + 1, 4) < 2
    z_mate = (me_s + PER_Z * (1 - 2 * lax.rem(layer, 2)), me_t)
    seat = lax.rem(me_s, PER_Z)
    base = me_s - seat
    far_base = n_sec - PER_Z - base
    across = (far_base + seat, me_t)
    lower = me_s < n_sec // 2

    def first_row(quarter):
        return pl.multiple_of(112 * quarter + 16 * (quarter // 2), 16)

    load_stash = pltpu.make_async_copy(stash_in, stash_ref, loads.at[0])
    load_fwd = pltpu.make_async_copy(fwd_in, fwd_ref, loads.at[1])
    load_og = pltpu.make_async_copy(og_in, og_ref, loads.at[2])
    small = [
        pltpu.make_async_copy(src, dst, loads.at[3 + i])
        for i, (src, dst) in enumerate(((read_in, read_ref), (write_in, write_ref), (gain_in, gain_ref)))
    ]
    load_stash.start()
    load_fwd.start()
    load_og.start()
    for load in small:
        load.start()

    barrier = pltpu.get_barrier_semaphore()

    def greet(device):
        pl.semaphore_signal(barrier, inc=1, device_id=device, device_id_type=MESH)

    greet(partner)
    greet(z_mate)
    greet(across)
    for step in range(1, PER_Z):
        greet((base + lax.rem(seat + step, PER_Z), me_t))
    greet((lax.rem(me_s + 1, n_sec), me_t))
    greet((lax.rem(me_s + n_sec - 1, n_sec), me_t))

    def greet_peer(step, carry):
        greet((me_s, lax.rem(me_t + step, n_ten)))
        return carry

    lax.fori_loop(1, n_ten, greet_peer, 0)

    def swaps(section, is_lower):
        return (write_ref[section] < 1) != is_lower

    def partner_reads(section, is_lower):
        return (read_ref[n_sec - 1 - section] < 1) == is_lower

    def overflow(first, is_lower):
        both = [
            jnp.where(
                jnp.logical_and(swaps(first + i, is_lower), partner_reads(first + i, is_lower)), 1, 0
            )
            for i in range(PER_Z)
        ]
        ranks = [sum(both[:i]) if i else jnp.int32(0) for i in range(PER_Z)]
        return both, ranks

    for load in small:
        load.wait()
    load_stash.wait()
    load_fwd.wait()
    sends_stash = partner_reads(me_s, lower)
    for i in range(3):
        pay_ref[i] = jnp.where(sends_stash, stash_ref[i], fwd_ref[i])
    both_out, rank_out = overflow(base, lower)
    both_in, rank_in = overflow(far_base, jnp.logical_not(lower))
    pl.semaphore_wait(barrier, n_ten + 7)

    def copy_to(src, dst, send, recv, device):
        return pltpu.make_async_remote_copy(
            src_ref=src, dst_ref=dst, send_sem=send, recv_sem=recv, device_id=device, device_id_type=MESH
        )

    def stash_copy(h):
        return copy_to(
            pay_ref.at[:, :, cols(h)], got_s.at[:, :, cols(h)], s_send.at[h], s_recv.at[h], partner
        )

    def quarter_copy(step):
        other = lax.rem(seat + step, PER_Z)
        return copy_to(
            fwd_ref.at[:, pl.ds(first_row(other), PART), :], gathered.at[seat],
            q_send.at[step], q_recv.at[seat], (base + other, me_t),
        )

    def quarter_arrival(step):
        other = lax.rem(seat + step, PER_Z)
        return copy_to(
            fwd_ref.at[:, pl.ds(first_row(other), PART), :], gathered.at[other],
            q_send.at[step], q_recv.at[other], (base + other, me_t),
        )

    def cross_copy(i):
        return copy_to(packed.at[i], crossed.at[i], c_send.at[i], c_recv.at[i], across)

    def fan_copy(i, step):
        other = lax.rem(seat + step, PER_Z)
        return copy_to(
            fan.at[i, other], quarters.at[i, seat], d_send.at[i, step], d_recv.at[i, seat], (base + other, me_t)
        )

    def fan_arrival(i, step):
        other = lax.rem(seat + step, PER_Z)
        return copy_to(
            fan.at[i, other], quarters.at[i, other], d_send.at[i, step], d_recv.at[i, other], (base + other, me_t)
        )

    def grad_copy(h):
        return copy_to(
            grad_out.at[:, :, cols(h)], grad_ref.at[:, :, cols(h)], g_send.at[h], g_recv.at[h], down
        )

    def act_copy():
        return copy_to(act_out, act_ref, a_send.at[0], a_recv.at[0], up)

    def spread(tiles, send, recv):
        def start(step, carry):
            peer = lax.rem(me_t + step, n_ten)
            copy_to(tiles.at[me_t], tiles.at[me_t], send.at[step], recv.at[me_t], (me_s, peer)).start()
            return carry

        lax.fori_loop(1, n_ten, start, 0)

    def collect(tiles, send, recv):
        def finish(step, carry):
            peer = lax.rem(me_t + step, n_ten)
            copy_to(tiles.at[me_t], tiles.at[me_t], send.at[step], recv.at[me_t], (me_s, peer)).wait_send()
            copy_to(tiles.at[peer], tiles.at[peer], send.at[step], recv.at[peer], (me_s, peer)).wait_recv()
            return carry

        lax.fori_loop(1, n_ten, finish, 0)
        return jnp.sum(tiles[...], axis=0)

    def token_sums(tile, row, partial):
        wide[0:length, :] = partial
        for block in range(4):
            summed = jnp.sum(jnp.transpose(wide[block * HD : (block + 1) * HD, :]), axis=0, keepdims=True)
            tile[row + block : row + block + 1, :] = summed

    def per_token(rows):
        blocks = [
            jnp.transpose(jnp.broadcast_to(rows[b : b + 1, :], (HD, HD))) for b in range(4)
        ]
        return jnp.concatenate(blocks, axis=0)[0:length, :]

    for h in range(heads):
        stash_copy(h).start()

    for step in range(1, PER_Z):
        quarter_copy(step).start()

    wide[...] = jnp.zeros_like(wide)
    tiles_f[me_t] = jnp.zeros((8, HD), F32)

    load_og.wait()
    squares = jnp.zeros((length, HD), F32)
    for h in range(heads):
        unused_a, unused_b, out = attend(fwd_ref[0, :, cols(h)], fwd_ref[1, :, cols(h)], fwd_ref[2, :, cols(h)])
        att_f[:, cols(h)] = out
        squares += out * out
    token_sums(part, 0, squares)
    tiles_f[me_t, 0:4, :] = part[0:4, :]
    spread(tiles_f, pf_send, pf_recv)
    total = collect(tiles_f, pf_send, pf_recv)
    inv_fwd = per_token(lax.rsqrt(total[0:4, :] / width_all + NORM_EPS))
    for h in range(heads):
        act_out[:, cols(h)] = (att_f[:, cols(h)] * inv_fwd * gain_ref[cols(h)][None, :]).astype(BF16)
    pl.when(has_up)(lambda: act_copy().start())

    @pl.when(jnp.logical_not(has_down))
    def _():
        zeros[...] = jnp.zeros_like(zeros)
        blank = pltpu.make_async_copy(zeros.at[0], act_ref, loads.at[6])
        blank.start()
        blank.wait()

    @pl.when(jnp.logical_not(has_up))
    def _():
        zeros[...] = jnp.zeros_like(zeros)
        blank = pltpu.make_async_copy(zeros, grad_ref, loads.at[6])
        blank.start()
        blank.wait()

    gathered[seat] = fwd_ref[:, pl.ds(first_row(seat), PART), :]
    for step in range(1, PER_Z):
        quarter_copy(step).wait_send()
        quarter_arrival(step).wait_recv()
    for slot in range(slots):
        member = sum(
            jnp.where(jnp.logical_and(both_out[i] == 1, rank_out[i] == slot), i, 0) for i in range(1, PER_Z)
        )
        for i in range(3):
            packed[i, slot] = gathered[member, i]

    own_read = (read_ref[me_s] < 1) == lower
    own_write = (write_ref[me_s] < 1) == lower
    squares = jnp.zeros((length, HD), F32)
    products = jnp.zeros((length, HD), F32)
    for h in range(heads):
        if h == heads - 1:
            for other in range(heads):
                stash_copy(other).wait_send()

            @pl.when(next_to_middle)
            def _():
                pl.semaphore_signal(go_sem, inc=1, device_id=z_mate, device_id_type=MESH)
                for i in range(3):
                    cross_copy(i).start()

        stash_copy(h).wait_recv()
        for part_at in range(3):
            back_ref[part_at, :, cols(h)] = jnp.where(
                own_read, stash_ref[part_at, :, cols(h)], got_s[part_at, :, cols(h)]
            )
        probs, low, out = attend(back_ref[0, :, cols(h)], back_ref[1, :, cols(h)], back_ref[2, :, cols(h)])
        probs_ref[h] = probs
        low_ref[h] = low
        att_b[:, cols(h)] = out
        squares += out * out
        products += og_ref[:, cols(h)].astype(F32) * gain_ref[cols(h)][None, :] * out
    token_sums(part, 0, squares)
    token_sums(part, 4, products)
    tiles_b[me_t] = part[...]
    spread(tiles_b, pb_send, pb_recv)
    total = collect(tiles_b, pb_send, pb_recv)
    inv = lax.rsqrt(total[0:4, :] / width_all + NORM_EPS)
    inv_back = per_token(inv)
    pull = per_token(inv * inv * inv * (total[4:8, :] / width_all))
    for h in range(heads):
        out = att_b[:, cols(h)]
        scaled = og_ref[:, cols(h)].astype(F32) * gain_ref[cols(h)][None, :]
        g_low = (inv_back * scaled - out * pull).astype(BF16)
        grad_probs = nt(g_low, back_ref[2, :, cols(h)])
        delta = jnp.sum(g_low.astype(F32) * out, axis=-1, keepdims=True)
        grad_scores = (probs_ref[h] * (grad_probs - delta) * SCALE).astype(BF16)
        grad_out[0, :, cols(h)] = nn(grad_scores, back_ref[1, :, cols(h)]).astype(BF16)
        grad_out[1, :, cols(h)] = tn(grad_scores, back_ref[0, :, cols(h)]).astype(BF16)
        grad_out[2, :, cols(h)] = tn(low_ref[h], g_low).astype(BF16)
        pl.when(has_down)(lambda: grad_copy(h).start())

    @pl.when(jnp.logical_not(next_to_middle))
    def _():
        pl.semaphore_wait(go_sem, 1)
        for i in range(3):
            cross_copy(i).start()

    for i in range(3):
        cross_copy(i).wait()
        for member in range(PER_Z):
            slot = jnp.minimum(rank_in[PER_Z - 1 - member], slots - 1)
            quarter = crossed[i, 0]
            for other in range(1, slots):
                quarter = jnp.where(slot == other, crossed[i, other], quarter)
            fan[i, member] = quarter
        for step in range(1, PER_Z):
            fan_copy(i, step).start()

    for i in range(3):
        quarters[i, seat] = fan[i, seat]
        for step in range(1, PER_Z):
            fan_arrival(i, step).wait_recv()
        for quarter in range(PER_Z):
            rows = pl.ds(112 * quarter + 16 * (quarter // 2), PART)
            new_ref[i, rows, :] = jnp.where(
                own_write,
                fwd_ref[i, rows, :],
                jnp.where(own_read, got_s[i, rows, :], quarters[i, quarter]),
            )
    for i in range(3):
        for step in range(1, PER_Z):
            fan_copy(i, step).wait_send()

    store = pltpu.make_async_copy(new_ref, new_out, loads.at[7])
    store.start()

    @pl.when(has_up)
    def _():
        act_copy().wait_send()
        for h in range(heads):
            grad_copy(h).wait_recv()

    @pl.when(has_down)
    def _():
        act_copy().wait_recv()
        for h in range(heads):
            grad_copy(h).wait_send()

    store.wait()


def shards(fwd_qkv, stash, out_grad, norm_gain, read_slot, write_slot):
    n_sec = lax.axis_size("section")
    n_ten = lax.axis_size("tensor")
    three, length, width = fwd_qkv.shape[1:]
    heads = width // HD
    dma = pltpu.SemaphoreType.DMA
    triple = pltpu.VMEM((three, length, width), BF16)

    def call(slots):
        return pl.pallas_call(
            functools.partial(kernel, n_sec, n_ten, float(width * n_ten), slots),
            out_shape=(
                jax.ShapeDtypeStruct((length, width), BF16),
                jax.ShapeDtypeStruct((three, length, width), BF16),
                jax.ShapeDtypeStruct((three, length, width), BF16),
            ),
            in_specs=[pl.BlockSpec(memory_space=pl.ANY)] * 6,
            out_specs=(pl.BlockSpec(memory_space=pl.ANY),) * 3,
            scratch_shapes=[
                triple, triple,
                pltpu.SMEM(read_slot.shape, jnp.int32),
                pltpu.SMEM(write_slot.shape, jnp.int32),
                pltpu.VMEM(norm_gain.shape, F32),
                triple, triple, pltpu.VMEM((length, width), BF16),
                triple, triple, triple,
                pltpu.VMEM((PER_Z, three, PART, width), BF16),
                pltpu.VMEM((three, slots, PART, width), BF16),
                pltpu.VMEM((three, slots, PART, width), BF16),
                pltpu.VMEM((three, PER_Z, PART, width), BF16),
                pltpu.VMEM((three, PER_Z, PART, width), BF16),
                pltpu.VMEM((length, width), BF16),
                triple,
                pltpu.VMEM((length, width), F32),
                pltpu.VMEM((length, width), F32),
                pltpu.VMEM((heads, length, length), F32),
                pltpu.VMEM((heads, length, length), BF16),
                pltpu.VMEM((8, HD), F32),
                pltpu.VMEM((4 * HD, HD), F32),
                pltpu.VMEM((n_ten, 8, HD), F32),
                pltpu.VMEM((n_ten, 8, HD), F32),
                dma((heads,)), dma((heads,)),
                dma((PER_Z,)), dma((PER_Z,)), dma((three,)), dma((three,)), dma((three, PER_Z)), dma((three, PER_Z)),
                dma((heads,)), dma((heads,)), dma((1,)), dma((1,)),
                dma((n_ten,)), dma((n_ten,)), dma((n_ten,)), dma((n_ten,)),
                dma((8,)), pltpu.SemaphoreType.REGULAR,
            ],
            compiler_params=pltpu.CompilerParams(
                collective_id=slots - LEAST, has_side_effects=True, vmem_limit_bytes=56 * 1024 * 1024
            ),
            name="slot%d" % slots,
        )

    here = jnp.arange(n_sec, dtype=jnp.int32)
    lower = here < n_sec // 2
    both = ((write_slot < 1) != lower) & ((jnp.flip(read_slot) < 1) == lower)
    most = jnp.max(jnp.sum(both.astype(jnp.int32).reshape(-1, PER_Z), axis=1))
    act, grads, new = lax.switch(
        jnp.maximum(most, LEAST) - LEAST,
        [call(slots) for slots in range(LEAST, PER_Z + 1)],
        read_slot, write_slot, fwd_qkv[0], stash[0, 0], out_grad[0], norm_gain,
    )
    return act[None], grads[None], new[None, None]


def solution(mesh):
    in_specs = (
        P("section", None, None, "tensor"),
        P("section", None, None, None, "tensor"),
        P("section", None, "tensor"),
        P("tensor"),
        P(),
        P(),
    )
    out_specs = (
        P("section", None, "tensor"),
        P("section", None, None, "tensor"),
        P("section", None, None, None, "tensor"),
    )
    return jax.shard_map(shards, mesh=mesh, in_specs=in_specs, out_specs=out_specs, check_vma=False)
```

```python
import functools

import jax
import jax.numpy as jnp
from jax import lax
from jax.experimental import pallas as pl
from jax.experimental.pallas import tpu as pltpu
from jax.sharding import PartitionSpec as P

HD = 128
NORM_EPS = 1e-05
SCALE = HD ** (-0.5)
PER_Z = 4
PLANS = ((2, 1), (4, 2), (4, 3), (1, 1))
PART_ROWS = {1: 480, 2: 240, 4: 128}
MESH = pl.DeviceIdType.MESH
F32 = jnp.float32
BF16 = jnp.bfloat16


def cols(head):
    return pl.ds(head * HD, HD)


def nt(a, b):
    return lax.dot_general(a, b, (((1,), (1,)), ((), ())), preferred_element_type=F32)


def nn(a, b):
    return lax.dot_general(a, b, (((1,), (0,)), ((), ())), preferred_element_type=F32)


def tn(a, b):
    return lax.dot_general(a, b, (((0,), (0,)), ((), ())), preferred_element_type=F32)


def attend(q, k, v):
    length = q.shape[0]
    scores = nt(q, k) * SCALE
    rows = lax.broadcasted_iota(jnp.int32, (length, length), 0)
    keys = lax.broadcasted_iota(jnp.int32, (length, length), 1)
    scores = jnp.where(rows >= keys, scores, F32(-1e30))
    terms = jnp.exp(scores - jnp.max(scores, axis=-1, keepdims=True))
    probs = terms * (1.0 / jnp.sum(terms, axis=-1, keepdims=True))
    low = probs.astype(BF16)
    return probs, low, nn(low, v)


def kernel(
    n_sec, n_ten, width_all, group, slots,
    read_in, write_in, fwd_in, stash_in, og_in, gain_in,
    act_ref, grad_ref, new_out,
    new_ref, zeros, read_ref, write_ref, gain_ref, fwd_ref, stash_ref, og_ref, pay_ref, got_s, back_ref, gathered, packed, staged, crossed, fan, pieces, act_out, grad_out, att_f, att_b, probs_ref, low_ref, part, wide, tiles_f, tiles_b,
    s_send, s_recv, q_send, q_recv, x_send, x_recv, c_send, c_recv, d_send, d_recv, g_send, g_recv, a_send, a_recv, pf_send, pf_recv, pb_send, pb_recv, loads, go_sem,
):
    length = og_ref.shape[0]
    heads = og_ref.shape[1] // HD
    me_s = lax.axis_index("section")
    me_t = lax.axis_index("tensor")
    partner = (n_sec - 1 - me_s, me_t)
    up = (me_s + 1, me_t)
    down = (me_s - 1, me_t)
    has_up = me_s < n_sec - 1
    has_down = me_s > 0
    layer = me_s // PER_Z
    next_to_middle = lax.rem(layer + 1, 4) < 2
    z_mate = (me_s + PER_Z * (1 - 2 * lax.rem(layer, 2)), me_t)
    seat = lax.rem(me_s, group)
    base = me_s - seat
    far_base = n_sec - group - base
    across = (n_sec - PER_Z * (layer + 1) + lax.rem(me_s, PER_Z), me_t)
    beside = (me_s + 2 * (1 - 2 * lax.rem(me_s // 2, 2)), me_t)
    lower = me_s < n_sec // 2

    part_rows = PART_ROWS[group]

    def first_row(piece):
        return 112 * piece + 16 * (piece // 2) if group == 4 else part_rows * piece

    def rows_of(piece):
        return pl.ds(pl.multiple_of(first_row(piece), 16), part_rows)

    load_stash = pltpu.make_async_copy(stash_in, stash_ref, loads.at[0])
    load_fwd = pltpu.make_async_copy(fwd_in, fwd_ref, loads.at[1])
    load_og = pltpu.make_async_copy(og_in, og_ref, loads.at[2])
    small = [
        pltpu.make_async_copy(src, dst, loads.at[3 + i])
        for i, (src, dst) in enumerate(((read_in, read_ref), (write_in, write_ref), (gain_in, gain_ref)))
    ]
    load_stash.start()
    load_fwd.start()
    load_og.start()
    for load in small:
        load.start()

    barrier = pltpu.get_barrier_semaphore()

    def greet(device):
        pl.semaphore_signal(barrier, inc=1, device_id=device, device_id_type=MESH)

    greet(partner)
    greet(z_mate)
    greet(across)
    if group == 2:
        greet(beside)
    for step in range(1, group):
        greet((base + lax.rem(seat + step, group), me_t))
    greet((lax.rem(me_s + 1, n_sec), me_t))
    greet((lax.rem(me_s + n_sec - 1, n_sec), me_t))

    def greet_peer(step, carry):
        greet((me_s, lax.rem(me_t + step, n_ten)))
        return carry

    lax.fori_loop(1, n_ten, greet_peer, 0)

    def swaps(section, is_lower):
        return (write_ref[section] < 1) != is_lower

    def partner_reads(section, is_lower):
        return (read_ref[n_sec - 1 - section] < 1) == is_lower

    def overflow(first, is_lower):
        both = [
            jnp.where(
                jnp.logical_and(swaps(first + i, is_lower), partner_reads(first + i, is_lower)), 1, 0
            )
            for i in range(group)
        ]
        ranks = [sum(both[:i]) if i else jnp.int32(0) for i in range(group)]
        return both, ranks

    for load in small:
        load.wait()
    load_stash.wait()
    load_fwd.wait()
    sends_stash = partner_reads(me_s, lower)
    for i in range(3):
        pay_ref[i] = jnp.where(sends_stash, stash_ref[i], fwd_ref[i])
    both_out, rank_out = overflow(base, lower)
    both_in, rank_in = overflow(far_base, jnp.logical_not(lower))
    pl.semaphore_wait(barrier, n_ten + 3 + group + (1 if group == 2 else 0))

    def copy_to(src, dst, send, recv, device):
        return pltpu.make_async_remote_copy(
            src_ref=src, dst_ref=dst, send_sem=send, recv_sem=recv, device_id=device, device_id_type=MESH
        )

    def stash_copy(h):
        return copy_to(
            pay_ref.at[:, :, cols(h)], got_s.at[:, :, cols(h)], s_send.at[h], s_recv.at[h], partner
        )

    def piece_copy(step):
        other = lax.rem(seat + step, group)
        return copy_to(
            fwd_ref.at[:, rows_of(other), :], gathered.at[seat],
            q_send.at[step], q_recv.at[seat], (base + other, me_t),
        )

    def piece_arrival(step):
        other = lax.rem(seat + step, group)
        return copy_to(
            fwd_ref.at[:, rows_of(other), :], gathered.at[other],
            q_send.at[step], q_recv.at[other], (base + other, me_t),
        )

    def cross_copy(i):
        if group == 1:
            return copy_to(fwd_ref.at[i], pieces.at[i, 0], c_send.at[i], c_recv.at[i], partner)
        ready = staged if group == 2 else packed
        return copy_to(ready.at[i], crossed.at[i], c_send.at[i], c_recv.at[i], across)

    def stage_copy(i):
        return copy_to(packed.at[i], staged.at[i], x_send.at[i], x_recv.at[i], beside)

    def fan_copy(i, step):
        other = lax.rem(seat + step, group)
        return copy_to(
            fan.at[i, other], pieces.at[i, seat], d_send.at[i, step], d_recv.at[i, seat], (base + other, me_t)
        )

    def fan_arrival(i, step):
        other = lax.rem(seat + step, group)
        return copy_to(
            fan.at[i, other], pieces.at[i, other], d_send.at[i, step], d_recv.at[i, other], (base + other, me_t)
        )

    def grad_copy(h):
        return copy_to(
            grad_out.at[:, :, cols(h)], grad_ref.at[:, :, cols(h)], g_send.at[h], g_recv.at[h], down
        )

    def act_copy():
        return copy_to(act_out, act_ref, a_send.at[0], a_recv.at[0], up)

    def spread(tiles, send, recv):
        def start(step, carry):
            peer = lax.rem(me_t + step, n_ten)
            copy_to(tiles.at[me_t], tiles.at[me_t], send.at[step], recv.at[me_t], (me_s, peer)).start()
            return carry

        lax.fori_loop(1, n_ten, start, 0)

    def collect(tiles, send, recv):
        def finish(step, carry):
            peer = lax.rem(me_t + step, n_ten)
            copy_to(tiles.at[me_t], tiles.at[me_t], send.at[step], recv.at[me_t], (me_s, peer)).wait_send()
            copy_to(tiles.at[peer], tiles.at[peer], send.at[step], recv.at[peer], (me_s, peer)).wait_recv()
            return carry

        lax.fori_loop(1, n_ten, finish, 0)
        return jnp.sum(tiles[...], axis=0)

    def token_sums(tile, row, partial):
        wide[0:length, :] = partial
        for block in range(4):
            summed = jnp.sum(jnp.transpose(wide[block * HD : (block + 1) * HD, :]), axis=0, keepdims=True)
            tile[row + block : row + block + 1, :] = summed

    def per_token(rows):
        blocks = [
            jnp.transpose(jnp.broadcast_to(rows[b : b + 1, :], (HD, HD))) for b in range(4)
        ]
        return jnp.concatenate(blocks, axis=0)[0:length, :]

    for h in range(heads):
        stash_copy(h).start()

    for step in range(1, group):
        piece_copy(step).start()

    wide[...] = jnp.zeros_like(wide)
    tiles_f[me_t] = jnp.zeros((8, HD), F32)

    load_og.wait()
    squares = jnp.zeros((length, HD), F32)
    for h in range(heads):
        unused_a, unused_b, out = attend(fwd_ref[0, :, cols(h)], fwd_ref[1, :, cols(h)], fwd_ref[2, :, cols(h)])
        att_f[:, cols(h)] = out
        squares += out * out
    token_sums(part, 0, squares)
    tiles_f[me_t, 0:4, :] = part[0:4, :]
    spread(tiles_f, pf_send, pf_recv)
    total = collect(tiles_f, pf_send, pf_recv)
    inv_fwd = per_token(lax.rsqrt(total[0:4, :] / width_all + NORM_EPS))
    for h in range(heads):
        act_out[:, cols(h)] = (att_f[:, cols(h)] * inv_fwd * gain_ref[cols(h)][None, :]).astype(BF16)
    pl.when(has_up)(lambda: act_copy().start())

    @pl.when(jnp.logical_not(has_down))
    def _():
        zeros[...] = jnp.zeros_like(zeros)
        blank = pltpu.make_async_copy(zeros.at[0], act_ref, loads.at[6])
        blank.start()
        blank.wait()

    @pl.when(jnp.logical_not(has_up))
    def _():
        zeros[...] = jnp.zeros_like(zeros)
        blank = pltpu.make_async_copy(zeros, grad_ref, loads.at[6])
        blank.start()
        blank.wait()

    if group > 1:
        gathered[seat] = fwd_ref[:, rows_of(seat), :]
    for step in range(1, group):
        piece_copy(step).wait_send()
        piece_arrival(step).wait_recv()
    for slot in range(slots if group > 1 else 0):
        member = sum(
            jnp.where(jnp.logical_and(both_out[i] == 1, rank_out[i] == slot), i, 0) for i in range(1, group)
        )
        for i in range(3):
            packed[i, slot] = gathered[member, i]
    if group == 2:
        for i in range(3):
            stage_copy(i).start()

    own_read = (read_ref[me_s] < 1) == lower
    own_write = (write_ref[me_s] < 1) == lower
    squares = jnp.zeros((length, HD), F32)
    products = jnp.zeros((length, HD), F32)
    for h in range(heads):
        if h == heads - 1:
            for other in range(heads):
                stash_copy(other).wait_send()
            if group == 2:
                for i in range(3):
                    stage_copy(i).wait()

            @pl.when(next_to_middle)
            def _():
                pl.semaphore_signal(go_sem, inc=1, device_id=z_mate, device_id_type=MESH)
                for i in range(3):
                    cross_copy(i).start()

        stash_copy(h).wait_recv()
        for part_at in range(3):
            back_ref[part_at, :, cols(h)] = jnp.where(
                own_read, stash_ref[part_at, :, cols(h)], got_s[part_at, :, cols(h)]
            )
        probs, low, out = attend(back_ref[0, :, cols(h)], back_ref[1, :, cols(h)], back_ref[2, :, cols(h)])
        probs_ref[h] = probs
        low_ref[h] = low
        att_b[:, cols(h)] = out
        squares += out * out
        products += og_ref[:, cols(h)].astype(F32) * gain_ref[cols(h)][None, :] * out
    token_sums(part, 0, squares)
    token_sums(part, 4, products)
    tiles_b[me_t] = part[...]
    spread(tiles_b, pb_send, pb_recv)
    total = collect(tiles_b, pb_send, pb_recv)
    inv = lax.rsqrt(total[0:4, :] / width_all + NORM_EPS)
    inv_back = per_token(inv)
    pull = per_token(inv * inv * inv * (total[4:8, :] / width_all))
    for h in range(heads):
        out = att_b[:, cols(h)]
        scaled = og_ref[:, cols(h)].astype(F32) * gain_ref[cols(h)][None, :]
        g_low = (inv_back * scaled - out * pull).astype(BF16)
        grad_probs = nt(g_low, back_ref[2, :, cols(h)])
        delta = jnp.sum(g_low.astype(F32) * out, axis=-1, keepdims=True)
        grad_scores = (probs_ref[h] * (grad_probs - delta) * SCALE).astype(BF16)
        grad_out[0, :, cols(h)] = nn(grad_scores, back_ref[1, :, cols(h)]).astype(BF16)
        grad_out[1, :, cols(h)] = tn(grad_scores, back_ref[0, :, cols(h)]).astype(BF16)
        grad_out[2, :, cols(h)] = tn(low_ref[h], g_low).astype(BF16)
        pl.when(has_down)(lambda: grad_copy(h).start())

    @pl.when(jnp.logical_not(next_to_middle))
    def _():
        pl.semaphore_wait(go_sem, 1)
        for i in range(3):
            cross_copy(i).start()

    for i in range(3):
        cross_copy(i).wait()
        for member in range(group if group > 1 else 0):
            slot = jnp.minimum(rank_in[group - 1 - member], slots - 1)
            found = crossed[i, 0]
            for other in range(1, slots):
                found = jnp.where(slot == other, crossed[i, other], found)
            fan[i, member] = found
        for step in range(1, group):
            fan_copy(i, step).start()

    for i in range(3):
        if group > 1:
            pieces[i, seat] = fan[i, seat]
        for step in range(1, group):
            fan_arrival(i, step).wait_recv()
        for piece in range(group):
            rows = pl.ds(first_row(piece), part_rows)
            new_ref[i, rows, :] = jnp.where(
                own_write,
                fwd_ref[i, rows, :],
                jnp.where(own_read, got_s[i, rows, :], pieces[i, piece]),
            )
    for i in range(3):
        for step in range(1, group):
            fan_copy(i, step).wait_send()

    store = pltpu.make_async_copy(new_ref, new_out, loads.at[7])
    store.start()

    @pl.when(has_up)
    def _():
        act_copy().wait_send()
        for h in range(heads):
            grad_copy(h).wait_recv()

    @pl.when(has_down)
    def _():
        act_copy().wait_recv()
        for h in range(heads):
            grad_copy(h).wait_send()

    store.wait()


def hand_over(a_in, b_in, c_in, a_out, b_out, c_out, sems):
    moves = [
        pltpu.make_async_copy(src, dst, sems.at[i])
        for i, (src, dst) in enumerate(((a_in, a_out), (b_in, b_out), (c_in, c_out)))
    ]
    for move in moves:
        move.start()
    for move in moves:
        move.wait()


def shards(fwd_qkv, stash, out_grad, norm_gain, read_slot, write_slot):
    n_sec = lax.axis_size("section")
    n_ten = lax.axis_size("tensor")
    three, length, width = fwd_qkv.shape[1:]
    heads = width // HD
    dma = pltpu.SemaphoreType.DMA
    triple = pltpu.VMEM((three, length, width), BF16)

    def call(plan, group, slots):
        part_rows = PART_ROWS[group]
        return pl.pallas_call(
            functools.partial(kernel, n_sec, n_ten, float(width * n_ten), group, slots),
            out_shape=(
                jax.ShapeDtypeStruct((length, width), BF16),
                jax.ShapeDtypeStruct((three, length, width), BF16),
                jax.ShapeDtypeStruct((three, length, width), BF16),
            ),
            in_specs=[pl.BlockSpec(memory_space=pl.ANY)] * 6,
            out_specs=(pl.BlockSpec(memory_space=pl.ANY),) * 3,
            scratch_shapes=[
                triple, triple,
                pltpu.SMEM(read_slot.shape, jnp.int32),
                pltpu.SMEM(write_slot.shape, jnp.int32),
                pltpu.VMEM(norm_gain.shape, F32),
                triple, triple, pltpu.VMEM((length, width), BF16),
                triple, triple, triple,
                pltpu.VMEM((group, three, part_rows, width), BF16),
                pltpu.VMEM((three, slots, part_rows, width), BF16),
                pltpu.VMEM((three, slots, part_rows, width), BF16),
                pltpu.VMEM((three, slots, part_rows, width), BF16),
                pltpu.VMEM((three, group, part_rows, width), BF16),
                pltpu.VMEM((three, group, part_rows, width), BF16),
                pltpu.VMEM((length, width), BF16),
                triple,
                pltpu.VMEM((length, width), F32),
                pltpu.VMEM((length, width), F32),
                pltpu.VMEM((heads, length, length), F32),
                pltpu.VMEM((heads, length, length), BF16),
                pltpu.VMEM((8, HD), F32),
                pltpu.VMEM((4 * HD, HD), F32),
                pltpu.VMEM((n_ten, 8, HD), F32),
                pltpu.VMEM((n_ten, 8, HD), F32),
                dma((heads,)), dma((heads,)),
                dma((group,)), dma((group,)), dma((three,)), dma((three,)), dma((three,)), dma((three,)), dma((three, group)), dma((three, group)),
                dma((heads,)), dma((heads,)), dma((1,)), dma((1,)),
                dma((n_ten,)), dma((n_ten,)), dma((n_ten,)), dma((n_ten,)),
                dma((8,)), pltpu.SemaphoreType.REGULAR,
            ],
            compiler_params=pltpu.CompilerParams(
                collective_id=plan, has_side_effects=True, vmem_limit_bytes=56 * 1024 * 1024
            ),
            name="slot%d_%d" % (group, slots),
        )

    here = jnp.arange(n_sec, dtype=jnp.int32)
    lower = here < n_sec // 2
    both = ((write_slot < 1) != lower) & ((read_slot < 1) != lower)
    word = jnp.uint32
    chips = jnp.sum(jnp.where(both, word(1) << (2 * (here // 2)).astype(word), word(0)))
    fours = (chips & word(0x33333333)) + ((chips >> word(2)) & word(0x33333333))
    steps = (chips & word(0xAAAAAAAA), (fours + word(0x11111111)) & word(0x44444444), fours & word(0x44444444))
    act, grads, new = lax.switch(
        sum((step != 0).astype(jnp.int32) for step in steps),
        [call(plan, group, slots) for plan, (group, slots) in enumerate(PLANS)],
        read_slot, write_slot, fwd_qkv[0], stash[0, 0], out_grad[0], norm_gain,
    )
    act, grads, new = pl.pallas_call(
        hand_over,
        out_shape=tuple(jax.ShapeDtypeStruct(x.shape, x.dtype) for x in (act, grads, new)),
        in_specs=[pl.BlockSpec(memory_space=pltpu.VMEM)] * 3,
        out_specs=(pl.BlockSpec(memory_space=pl.ANY),) * 3,
        scratch_shapes=[dma((3,))],
        compiler_params=pltpu.CompilerParams(vmem_limit_bytes=56 * 1024 * 1024),
        name="hand_over",
    )(act, grads, new)
    return act[None], grads[None], new[None, None]


def solution(mesh):
    in_specs = (
        P("section", None, None, "tensor"),
        P("section", None, None, None, "tensor"),
        P("section", None, "tensor"),
        P("tensor"),
        P(),
        P(),
    )
    out_specs = (
        P("section", None, "tensor"),
        P("section", None, None, "tensor"),
        P("section", None, None, None, "tensor"),
    )
    return jax.shard_map(shards, mesh=mesh, in_specs=in_specs, out_specs=out_specs, check_vma=False)
```
